256 devices in a mesh: dp: 32 (over z_hi, x, core), section: 8 (over z_lo, y).
Axes of the slice: x: 4, y: 4, z: 8 (z_hi: 4, z_lo: 2; z = z_hi * 2 + z_lo), core: 2. Of those that a mesh axis runs over, the one named last changes fastest.
Arguments:
- layer_inputs: bfloat16 [8, 8192, 4096], P('section', 'dp'), may hold values from -120 to 120
- output_grads: bfloat16 [8, 8192, 4096], P('section', 'dp'), may hold values from -120 to 120
- proj_in: bfloat16 [8, 4096, 64], P('section'), may hold values from -0.09375 to 0.09375
- proj_out: bfloat16 [8, 4096, 64], P('section'), may hold values from -0.09375 to 0.09375
- train_log: bfloat16 [8, 24576, 4096], P('section', 'dp'), may hold values from -6 to 6
- queries: bfloat16 [8, 1024, 4096], P('section', 'dp'), may hold values from -6 to 6
- query_owner: int32 [32], replicated, may hold values from 0 to 31, each once
Outputs:
- fresh_grads: bfloat16 [8, 32, 4096], P('section', 'dp')
- scores: float32 [1024, 24576], P('section', 'dp')
The draws below stay inside these ranges and needn't reach their ends.
Inputs may be any that keep to these rules, and one draw needn't show every extreme that they name: `query_owner`: each stored block holds exactly one query block.
All inputs are finite; a program needn't handle non-finite values.
Results may differ from the reference program's by a relative error of at most 0.0065.
Values may be sent and summed in bfloat16 or wider, within the bound.
No kernel may reach another device: no remote copies, remote signals or barrier semaphores. Data moves between devices by JAX's collectives and lax.ppermute only.
A program may use at most 128 MiB of HBM per device.

```python
import math
import jax
import jax.numpy as jnp
from jax import lax

D = 4096
R = 64
SEQ = 256
EXL = 768
NQ = 1024
LAYERS = 8
TOKENS = 8192
LOGGED = 24576
N_DP = 32


def spread_field(key, noise, low, high):
    row_key, col_key = jax.random.split(key)
    positions = jnp.arange(TOKENS, dtype=jnp.float32)
    rise = jnp.exp(math.log(3.0) * positions / TOKENS)
    row_scale = rise[None, :, None] * jnp.exp(jax.random.uniform(row_key, (LAYERS, TOKENS, 1), jnp.float32, math.log(0.5), math.log(2.0)))
    col_scale = jnp.exp(jax.random.uniform(col_key, (LAYERS, 1, D), jnp.float32, math.log(low), math.log(high)))
    return (noise * row_scale * col_scale).astype(jnp.bfloat16)


def draw_layer_inputs(key, part):
    key = jax.random.fold_in(key, 11)
    noise_key, field_key = jax.random.split(key)
    noise = jax.random.truncated_normal(noise_key, -4.0, 4.0, (LAYERS, TOKENS, D), jnp.float32)
    return spread_field(field_key, noise, 0.5, 5.0)


def draw_output_grads(key, part):
    key = jax.random.fold_in(key, 23)
    noise_key, field_key = jax.random.split(key)
    noise = jax.random.truncated_normal(noise_key, -4.0, 4.0, (LAYERS, TOKENS, D), jnp.float32)
    return spread_field(field_key, noise, 0.5, 5.0)


def block_scale(key, shape, cuts, least, largest):
    loudness = 1.0
    for axis_at, shards_of in cuts:
        heights = jax.random.uniform(jax.random.fold_in(jax.random.fold_in(key, 6), axis_at), (shards_of,), jnp.float32, least / len(cuts), largest / len(cuts))
        loudness = loudness * jnp.repeat(jnp.exp(heights), shape[axis_at] // shards_of).reshape((-1,) + (1,) * (len(shape) - 1 - axis_at))
    return loudness


def centred(own_key, extent, spread, bound, cuts=(), held_as=jnp.bfloat16):
    loudness = block_scale(own_key, extent, cuts, -0.22, 0.18) if cuts else 1.0
    array = jax.random.normal(own_key, extent, jnp.float32) * spread * loudness
    return jnp.minimum(jnp.maximum(array, -bound), bound).astype(held_as)


def setup_inputs(seed: int = 0) -> dict:
    splits = jax.random.split(jax.random.key(seed), 8)
    layer_inputs = draw_layer_inputs(jax.random.fold_in(splits[7], 71), 0)
    output_grads = draw_output_grads(jax.random.fold_in(splits[7], 71), 0)
    proj_in = centred(splits[2], (LAYERS, D, R), D ** -0.5, 0.09375, ((0, 8),))
    proj_out = centred(splits[3], (LAYERS, D, R), D ** -0.5, 0.09375, ((0, 8),))
    train_log = centred(splits[4], (LAYERS, LOGGED, R * R), 1.0, 6.0, ((0, 8), (1, 32)))
    queries = centred(splits[5], (LAYERS, NQ, R * R), 1.0, 6.0, ((0, 8), (1, 32)))
    query_owner = jax.random.permutation(splits[6], N_DP).astype(jnp.int32)
    return dict(layer_inputs=layer_inputs, output_grads=output_grads, proj_in=proj_in, proj_out=proj_out, train_log=train_log, queries=queries, query_owner=query_owner)


def damped_inverse(factor):
    size = factor.shape[0]
    eye = jnp.eye(size, dtype=factor.dtype)
    damped = factor + 0.1 * jnp.trace(factor) / size * eye
    lower = jnp.linalg.cholesky(damped)
    solved = lax.linalg.triangular_solve(lower, eye, left_side=True, lower=True)
    return jnp.dot(solved.T, solved, precision=lax.Precision.HIGHEST)

def condition(block, out_inverse, in_inverse):
    rank = out_inverse.shape[0]
    out_half = out_inverse.astype(jnp.bfloat16).astype(jnp.float32)
    in_half = in_inverse.astype(jnp.bfloat16).astype(jnp.float32)
    matrices = block.astype(jnp.float32).reshape(block.shape[0], rank, rank)
    left = jnp.einsum('ok,qki->qoi', out_half, matrices, precision=lax.Precision.HIGHEST)
    left = left.astype(jnp.bfloat16).astype(jnp.float32)
    both = jnp.einsum('qok,ki->qoi', left, in_half, precision=lax.Precision.HIGHEST)
    return both.reshape(block.shape[0], rank * rank).astype(jnp.bfloat16)

def reference(layer_inputs, output_grads, proj_in, proj_out, train_log, queries, query_owner):
    fresh_list = []
    total = jnp.zeros((NQ, EXL * N_DP), jnp.float32)
    for layer in range(LAYERS):
        acts = jnp.dot(layer_inputs[layer].astype(jnp.float32), proj_in[layer].astype(jnp.float32), preferred_element_type=jnp.float32).astype(jnp.bfloat16)
        grads = jnp.dot(output_grads[layer].astype(jnp.float32), proj_out[layer].astype(jnp.float32), preferred_element_type=jnp.float32).astype(jnp.bfloat16)
        acts_wide = acts.astype(jnp.float32).reshape(-1, SEQ, R)
        grads_wide = grads.astype(jnp.float32).reshape(-1, SEQ, R)
        per_example = jnp.einsum('eso,esi->eoi', grads_wide, acts_wide, precision=lax.Precision.HIGHEST)
        fresh_list.append((per_example / SEQ).reshape(-1, R * R).astype(jnp.bfloat16))
        in_factor = jnp.dot(acts.T.astype(jnp.float32), acts.astype(jnp.float32), preferred_element_type=jnp.float32) / TOKENS
        out_factor = jnp.dot(grads.T.astype(jnp.float32), grads.astype(jnp.float32), preferred_element_type=jnp.float32) / TOKENS
        conditioned = condition(queries[layer], damped_inverse(out_factor), damped_inverse(in_factor))
        ordered = conditioned.reshape(N_DP, NQ // N_DP, R * R)[query_owner].reshape(NQ, R * R)
        total = total + jnp.dot(ordered.astype(jnp.float32), train_log[layer].T.astype(jnp.float32), preferred_element_type=jnp.float32)
    return (jnp.stack(fresh_list), total)
```

```python
import jax
import jax.numpy as jnp
from jax import lax
from jax.sharding import PartitionSpec as P

SEQ = 256
DP = ("zh", "x", "core")
SECTION = ("zl", "y")


def damped_inverse(factor):
    size = factor.shape[0]
    eye = jnp.eye(size, dtype=factor.dtype)
    damped = factor + 0.1 * jnp.trace(factor) / size * eye
    lower = jnp.linalg.cholesky(damped)
    solved = lax.linalg.triangular_solve(lower, eye, left_side=True, lower=True)
    return jnp.dot(solved.T, solved, precision=lax.Precision.HIGHEST)


def condition(block, out_half, in_half):
    rank = out_half.shape[0]
    matrices = block.reshape(block.shape[0], rank, rank)
    left = jnp.einsum("ok,qki->qoi", out_half, matrices, preferred_element_type=jnp.float32).astype(
        jnp.bfloat16
    )
    both = jnp.einsum("qok,ki->qoi", left, in_half, preferred_element_type=jnp.float32)
    return both.reshape(block.shape[0], rank * rank).astype(jnp.bfloat16)


def on_device(layer_inputs, output_grads, proj_in, proj_out, train_log, queries, query_owner):
    rank = proj_in.shape[2]
    local_tokens = layer_inputs.shape[1]
    total_tokens = local_tokens * lax.axis_size(DP)
    examples = local_tokens // SEQ
    layer = 0
    acts = jnp.dot(layer_inputs[layer], proj_in[layer], preferred_element_type=jnp.float32).astype(
        jnp.bfloat16
    )
    grads = jnp.dot(
        output_grads[layer], proj_out[layer], preferred_element_type=jnp.float32
    ).astype(jnp.bfloat16)
    per_example = lax.dot_general(
        grads.reshape(examples, SEQ, rank),
        acts.reshape(examples, SEQ, rank),
        (((1,), (1,)), ((0,), (0,))),
        preferred_element_type=jnp.float32,
    )
    fresh_list = [(per_example / SEQ).reshape(examples, rank * rank).astype(jnp.bfloat16)]
    in_list = [
        lax.dot_general(acts, acts, (((0,), (0,)), ((), ())), preferred_element_type=jnp.float32)
    ]
    out_list = [
        lax.dot_general(grads, grads, (((0,), (0,)), ((), ())), preferred_element_type=jnp.float32)
    ]
    fresh_grads = jnp.stack(fresh_list)
    sums = jnp.concatenate([in_list[0], out_list[0]], axis=1)
    for axis in ("core", "x", "zh"):
        size = lax.axis_size(axis)
        stride = 1
        while stride < size:
            sums = sums + lax.ppermute(sums, axis, [(i, i ^ stride) for i in range(size)])
            stride *= 2
    in_half = damped_inverse(sums[:, :rank] / total_tokens).astype(jnp.bfloat16)
    out_half = damped_inverse(sums[:, rank:] / total_tokens).astype(jnp.bfloat16)
    block_rows = queries.shape[1]
    dp_count = lax.axis_size(DP)
    conditioned = jnp.stack([condition(queries[0], out_half, in_half)])
    block = lax.all_gather(conditioned, DP, axis=1, tiled=True)
    layer = 0
    total = lax.dot_general(
        block[layer], train_log[layer], (((1,), (1,)), ((), ())), preferred_element_type=jnp.float32
    )
    ordered = jnp.take(
        total.astype(jnp.bfloat16).reshape(dp_count, block_rows, total.shape[1]), query_owner, axis=0
    )
    parts = lax.axis_size(SECTION)
    ordered = ordered.reshape(parts, total.shape[0] // parts, total.shape[1])
    arrived = lax.all_to_all(ordered, SECTION, split_axis=0, concat_axis=0, tiled=True)
    scores = jnp.sum(arrived.astype(jnp.float32), axis=0)
    return (fresh_grads, scores)


def solution(mesh):
    fine = jax.sharding.Mesh(
        mesh.devices.reshape(4, 4, 2, 2, 4), ("zh", "x", "core", "zl", "y")
    )
    placed = (
        P(SECTION, DP, None),
        P(SECTION, DP, None),
        P(SECTION, None, None),
        P(SECTION, None, None),
        P(SECTION, DP, None),
        P(SECTION, DP, None),
        P(),
    )
    return jax.shard_map(
        on_device,
        mesh=fine,
        in_specs=placed,
        out_specs=(P(SECTION, DP, None), P(SECTION, DP)),
        check_vma=False,
    )
```

```python
import functools

import jax
import jax.numpy as jnp
from jax import lax
from jax.experimental import pallas as pl
from jax.experimental.pallas import tpu as pltpu
from jax.sharding import PartitionSpec as P

SEQ = 256
RANK = 64
DP = ("zh", "x", "core")
SECTION = ("zl", "y")

def shuffle_kernel(t_ref, x_ref, wide):
    rows = t_ref.shape[0]
    width = t_ref.shape[1]
    for j in range(width // 128):
        wide[128*j:128*j+128, :] = t_ref[:, 128*j:128*j+128].astype(jnp.float32).T
    for i in range(RANK):
        x_ref[RANK*i:RANK*i+RANK, :] = wide[pl.ds(i, RANK, stride=RANK), :].astype(jnp.bfloat16)
def shuffle(t):
    n,w=t.shape
    return pl.pallas_call(shuffle_kernel, grid=(n//128,),
        in_specs=[pl.BlockSpec((128,w),lambda j:(j,0))],
        out_specs=pl.BlockSpec((w,128),lambda j:(0,j)),
        out_shape=jax.ShapeDtypeStruct((w,n),jnp.bfloat16),
        scratch_shapes=[pltpu.VMEM((w,128),jnp.float32)],
        compiler_params=pltpu.CompilerParams(vmem_limit_bytes=32*2**20),
        cost_estimate=pl.CostEstimate(flops=2*n*w*64,bytes_accessed=4*n*w,transcendentals=0),
    )(t)
def weigh_kernel(x_ref, a_ref, b_ref, y_ref, lo, hi):
    halves=(lo,hi)
    a=a_ref[...]; b=b_ref[...]
    w=x_ref.shape[0]
    for g in range(w//256):
        y=jnp.dot(a, x_ref[256*g:256*g+256,:], preferred_element_type=jnp.float32)
        lo[256*g:256*g+256,:]=y[:,:128]
        hi[256*g:256*g+256,:]=y[:,128:]
    for g in range(w//256):
        parts=[]
        for k in range(4*g,4*g+4):
            parts.append(jnp.concatenate([h[pl.ds(k,RANK,stride=RANK),:] for h in halves],axis=1).astype(jnp.bfloat16))
        z=jnp.concatenate(parts,axis=0)
        y_ref[256*g:256*g+256,:]=jnp.dot(b,z,preferred_element_type=jnp.float32).astype(jnp.bfloat16)
def weigh(x,a,b):
    w,n=x.shape
    return pl.pallas_call(weigh_kernel, grid=(n//256,),
        in_specs=[pl.BlockSpec((w,256),lambda j:(0,j)),pl.BlockSpec((256,256),lambda j:(0,0)),pl.BlockSpec((256,256),lambda j:(0,0))],
        out_specs=pl.BlockSpec((w,256),lambda j:(0,j)),
        out_shape=jax.ShapeDtypeStruct((w,n),jnp.bfloat16),
        scratch_shapes=[pltpu.VMEM((w,128),jnp.float32)]*2,
        compiler_params=pltpu.CompilerParams(vmem_limit_bytes=32*2**20),
        cost_estimate=pl.CostEstimate(flops=4*n*w*256,bytes_accessed=4*n*w,transcendentals=0),
    )(x,a,b)
def blocks(m):
    four=jnp.concatenate([m]*4,axis=1)
    four=jnp.concatenate([four]*4,axis=0)
    r=lax.broadcasted_iota(jnp.int32,four.shape,0)//RANK
    c=lax.broadcasted_iota(jnp.int32,four.shape,1)//RANK
    return jnp.where(r==c,four,0.0).astype(jnp.bfloat16)
def inverse_kernel(tokens, s_ref, a_ref, b_ref):
    m=s_ref[...]/tokens
    row=lax.broadcasted_iota(jnp.int32,m.shape,0)
    lane=lax.broadcasted_iota(jnp.int32,m.shape,1)
    left=lane<RANK
    lcol=jnp.where(left,lane,lane-RANK)
    diag=jnp.where(row==lcol,m,0.0)
    tl=jnp.sum(jnp.where(left,diag,0.0)); tr=jnp.sum(jnp.where(left,0.0,diag))
    m=m+jnp.where(row==lcol,jnp.where(left,tl,tr)*(0.1/RANK),0.0)
    for k in range(RANK):
        pr=m[k:k+1,:]
        l1=left[:1]
        piv=jnp.where(l1,pr[:,k:k+1],pr[:,RANK+k:RANK+k+1])
        at=lcol==k
        scaled=jnp.where(at[:1],1.0,pr)/piv
        col=jnp.where(left,m[:,k:k+1],m[:,RANK+k:RANK+k+1])
        m=jnp.where(row==k,scaled,jnp.where(at,0.0,m)-col*scaled)
    inb=m[:,:RANK]; outb=m[:,RANK:]
    a_ref[...]=blocks(outb.T)
    b_ref[...]=blocks(inb)
def inverses(s,tokens):
    return pl.pallas_call(functools.partial(inverse_kernel,tokens),
        out_shape=[jax.ShapeDtypeStruct((256,256),jnp.bfloat16)]*2,
        cost_estimate=pl.CostEstimate(flops=64*64*128*2,bytes_accessed=300000,transcendentals=0),
    )(s)


def dp_sum(value):
    for axis in ("core", "x", "zh"):
        last = lax.axis_size(axis) - 1
        value = value + lax.ppermute(value, axis, [(i, i ^ 1) for i in range(last + 1)])
        if last > 1:
            value = value + lax.ppermute(value, axis, [(i, last - i) for i in range(last + 1)])
    return value


def on_device(layer_inputs, output_grads, proj_in, proj_out, train_log, queries, query_owner):
    local_tokens = layer_inputs.shape[1]
    total_tokens = local_tokens * lax.axis_size(DP)
    block = lax.all_gather(queries[0], DP, axis=0, tiled=True)
    acts = jnp.dot(layer_inputs[0], proj_in[0], preferred_element_type=jnp.float32).astype(
        jnp.bfloat16
    )
    grads = jnp.dot(output_grads[0], proj_out[0], preferred_element_type=jnp.float32).astype(
        jnp.bfloat16
    )
    down = (((0,), (0,)), ((), ()))
    in_sum = lax.dot_general(acts, acts, down, preferred_element_type=jnp.float32)
    out_sum = lax.dot_general(grads, grads, down, preferred_element_type=jnp.float32)
    sums = dp_sum(jnp.concatenate([in_sum, out_sum], axis=1))
    examples = local_tokens // SEQ
    per_example = lax.dot_general(
        grads.reshape(examples, SEQ, RANK),
        acts.reshape(examples, SEQ, RANK),
        (((1,), (1,)), ((0,), (0,))),
        preferred_element_type=jnp.float32,
    )
    fresh_grads = (per_example / SEQ).reshape(1, examples, RANK * RANK).astype(jnp.bfloat16)
    turned = shuffle(train_log[0])
    out_blocks, in_blocks = inverses(sums, total_tokens)
    weighed = weigh(turned, out_blocks, in_blocks)
    total = jnp.dot(block, weighed, preferred_element_type=jnp.float32).astype(jnp.bfloat16)
    count = query_owner.shape[0]
    ordered = jnp.take(
        total.reshape(count, total.shape[0] // count, total.shape[1]), query_owner, axis=0
    )
    parts = lax.axis_size(SECTION)
    ordered = ordered.reshape(parts, total.shape[0] // parts, total.shape[1])
    arrived = lax.all_to_all(ordered, SECTION, split_axis=0, concat_axis=0, tiled=True)
    scores = jnp.sum(arrived.astype(jnp.float32), axis=0)
    return (fresh_grads, scores)


def solution(mesh):
    fine = jax.sharding.Mesh(
        mesh.devices.reshape(4, 4, 2, 2, 4), ("zh", "x", "core", "zl", "y")
    )
    placed = (
        P(SECTION, DP, None),
        P(SECTION, DP, None),
        P(SECTION, None, None),
        P(SECTION, None, None),
        P(SECTION, DP, None),
        P(SECTION, DP, None),
        P(),
    )
    return jax.shard_map(
        on_device,
        mesh=fine,
        in_specs=placed,
        out_specs=(P(SECTION, DP, None), P(SECTION, DP)),
        check_vma=False,
    )
```

```python
import functools

import jax
import jax.numpy as jnp
from jax import lax
from jax.experimental import pallas as pl
from jax.experimental.pallas import tpu as pltpu
from jax.sharding import PartitionSpec as P

SEQ = 256
RANK = 64
DP = ("zh", "x", "core")
SECTION = ("zl", "y")

VMEM_BYTES = 60 * 2**20
LIGHT = pl.CostEstimate(flops=0, bytes_accessed=1024, transcendentals=0)


def params():
    return pltpu.CompilerParams(vmem_limit_bytes=VMEM_BYTES)


def shuffle_kernel(t_ref, *refs):
    x_ref, wide = refs[-2:]
    for j in range(t_ref.shape[1] // 128):
        lanes = slice(128 * j, 128 * j + 128)
        wide[lanes, :] = t_ref[:, lanes].astype(jnp.float32).T
    for i in range(RANK):
        x_ref[RANK * i : RANK * i + RANK, :] = wide[pl.ds(i, RANK, stride=RANK), :].astype(
            jnp.bfloat16
        )


def shuffle(t, first, count, held=None):
    n, width = t.shape
    specs = [pl.BlockSpec((128, width), lambda j: (j + first, 0))]
    return pl.pallas_call(
        shuffle_kernel,
        grid=(count,),
        in_specs=specs + ([] if held is None else [pl.BlockSpec(memory_space=pl.ANY)]),
        out_specs=pl.BlockSpec((width, 128), lambda j: (0, j + first)),
        out_shape=jax.ShapeDtypeStruct((width, n), jnp.bfloat16),
        input_output_aliases={} if held is None else {1: 0},
        scratch_shapes=[pltpu.VMEM((width, 128), jnp.float32)],
        compiler_params=params(),
        cost_estimate=LIGHT,
    )(*((t,) if held is None else (t, held)))


def score_kernel(moves, count, pos_ref, x_ref, a_ref, b_ref, *refs):
    pieces, y_ref = refs[:count], refs[count]
    rows, low, high, weighed, sems = refs[count + 1 :]
    copies = []
    for n, (piece, start, size, slot, half) in enumerate(moves):
        place = pl.multiple_of(pos_ref[slot] * 32 + half * 16, 16)
        copies.append(
            pltpu.make_async_copy(
                pieces[piece].at[pl.ds(start, size)], rows.at[pl.ds(place, size)], sems.at[n]
            )
        )
    first = pl.program_id(0) == 0

    @pl.when(first)
    def _():
        for copy in copies:
            copy.start()

    a, b = a_ref[...], b_ref[...]
    width = x_ref.shape[0]
    for g in range(width // 256):
        band = slice(256 * g, 256 * g + 256)
        y = jnp.dot(a, x_ref[band, :], preferred_element_type=jnp.float32)
        low[band, :] = y[:, :128]
        high[band, :] = y[:, 128:]
    for g in range(width // 256):
        parts = []
        for k in range(4 * g, 4 * g + 4):
            pair = [half[pl.ds(k, RANK, stride=RANK), :] for half in (low, high)]
            parts.append(jnp.concatenate(pair, axis=1).astype(jnp.bfloat16))
        z = jnp.concatenate(parts, axis=0)
        weighed[256 * g : 256 * g + 256, :] = jnp.dot(
            b, z, preferred_element_type=jnp.float32
        ).astype(jnp.bfloat16)

    @pl.when(first)
    def _():
        for copy in copies:
            copy.wait()

    tall = 256
    for g in range(rows.shape[0] // tall):
        band = slice(tall * g, tall * g + tall)
        y_ref[band, :] = jnp.dot(
            rows[band, :], weighed[...], preferred_element_type=jnp.float32
        ).astype(jnp.bfloat16)


def score(pieces, moves, pos, x, a, b):
    width, n = x.shape
    total = sum(piece.shape[0] for piece in pieces)
    small = pl.BlockSpec((256, 256), lambda j: (0, 0))
    return pl.pallas_call(
        functools.partial(score_kernel, moves, len(pieces)),
        grid=(n // 256,),
        in_specs=[
            pl.BlockSpec(memory_space=pltpu.SMEM),
            pl.BlockSpec((width, 256), lambda j: (0, j)),
            small,
            small,
        ]
        + [pl.BlockSpec(memory_space=pl.ANY)] * len(pieces),
        out_specs=pl.BlockSpec((total, 256), lambda j: (0, j)),
        out_shape=jax.ShapeDtypeStruct((total, n), jnp.bfloat16),
        scratch_shapes=[
            pltpu.VMEM((total, width), jnp.bfloat16),
            pltpu.VMEM((width, 128), jnp.float32),
            pltpu.VMEM((width, 128), jnp.float32),
            pltpu.VMEM((width, 256), jnp.bfloat16),
            pltpu.SemaphoreType.DMA((len(moves),)),
        ],
        compiler_params=params(),
        cost_estimate=LIGHT,
    )(pos, x, a, b, *pieces)


def blocks(m):
    four=jnp.concatenate([m]*4,axis=1)
    four=jnp.concatenate([four]*4,axis=0)
    r=lax.broadcasted_iota(jnp.int32,four.shape,0)//RANK
    c=lax.broadcasted_iota(jnp.int32,four.shape,1)//RANK
    return jnp.where(r==c,four,0.0).astype(jnp.bfloat16)
def inverse_kernel(tokens, s_ref, a_ref, b_ref):
    m=s_ref[...]/tokens
    row=lax.broadcasted_iota(jnp.int32,m.shape,0)
    lane=lax.broadcasted_iota(jnp.int32,m.shape,1)
    left=lane<RANK
    lcol=jnp.where(left,lane,lane-RANK)
    diag=jnp.where(row==lcol,m,0.0)
    tl=jnp.sum(jnp.where(left,diag,0.0)); tr=jnp.sum(jnp.where(left,0.0,diag))
    m=m+jnp.where(row==lcol,jnp.where(left,tl,tr)*(0.1/RANK),0.0)
    for k in range(RANK):
        pr=m[k:k+1,:]
        l1=left[:1]
        piv=jnp.where(l1,pr[:,k:k+1],pr[:,RANK+k:RANK+k+1])
        at=lcol==k
        scaled=jnp.where(at[:1],1.0,pr)/piv
        col=jnp.where(left,m[:,k:k+1],m[:,RANK+k:RANK+k+1])
        m=jnp.where(row==k,scaled,jnp.where(at,0.0,m)-col*scaled)
    inb=m[:,:RANK]; outb=m[:,RANK:]
    a_ref[...]=blocks(outb.T)
    b_ref[...]=blocks(inb)
def inverses(s,tokens):
    return pl.pallas_call(functools.partial(inverse_kernel,tokens),
        out_shape=[jax.ShapeDtypeStruct((256,256),jnp.bfloat16)]*2,
        cost_estimate=LIGHT,
    )(s)


def shift(value, axis, step):
    size = lax.axis_size(axis)
    return lax.ppermute(value, axis, [(i, (i + step) % size) for i in range(size)])


def swap(value, axis, way):
    last = lax.axis_size(axis) - 1
    pairs = [(i, i ^ 1 if way == 0 else last - i) for i in range(last + 1)]
    return value + lax.ppermute(value, axis, pairs)


def forward(behind, ahead, axis):
    half = behind.shape[0] // 2
    return [shift(behind[:half], axis, 1), shift(ahead[half:], axis, -1)]


def layout():
    pair = [(0, 32, 3, 0), (32, 32, 1, 0)]
    far = [(0, 32, 2, 0)]
    groups = [(turn, [(0, 32, 0, 0)]) for turn in (0, 3, 1, 2)]
    groups += [(turn, pair) for turn in (0, 3, 1)] + [(2, [(0, 32, 3, 0)]), (2, [(0, 32, 1, 0)])]
    groups += [(turn, far) for turn in (0, 3, 1)] + [(2, [(0, 16, 2, 0)]), (2, [(0, 16, 2, 1)])]
    moves = []
    for other in range(2):
        for n, (turn, runs) in enumerate(groups):
            for start, size, climb, half in runs:
                slot = (climb * 4 + turn) * 2 + other
                moves.append((other * len(groups) + n, start, size, slot, half))
    return moves


def block_ids():
    zh, x, core = (lax.axis_index(axis) for axis in DP)
    ids = []
    for climb in range(4):
        for turn in range(4):
            for other in range(2):
                ids.append((((zh + climb) % 4) * 4 + (x + turn) % 4) * 2 + (core + other) % 2)
    return jnp.stack(ids)


def on_device(layer_inputs, output_grads, proj_in, proj_out, train_log, queries, query_owner):
    local_tokens = layer_inputs.shape[1]
    total_tokens = local_tokens * lax.axis_size(DP)
    hold = lax.optimization_barrier
    own, train = queries[0], train_log[0]
    behind, ahead = shift(own, "zh", 1), shift(own, "zh", -1)
    near = [own] + [shift(own, "x", step) for step in (1, -1, 2)]

    acts = jnp.dot(layer_inputs[0], proj_in[0], preferred_element_type=jnp.float32).astype(
        jnp.bfloat16
    )
    grads = jnp.dot(output_grads[0], proj_out[0], preferred_element_type=jnp.float32).astype(
        jnp.bfloat16
    )
    down = (((0,), (0,)), ((), ()))
    in_sum = lax.dot_general(acts, acts, down, preferred_element_type=jnp.float32)
    out_sum = lax.dot_general(grads, grads, down, preferred_element_type=jnp.float32)
    sums = swap(jnp.concatenate([in_sum, out_sum], axis=1), "core", 0)
    sums, train = hold((swap(sums, "x", 0), train))
    turned = shuffle(train, 0, 2)
    sums, turned, behind, ahead = hold((swap(sums, "x", 1), turned, behind, ahead))
    far = forward(behind, ahead, "zh")
    pair = jnp.concatenate([behind, ahead], axis=0)
    pairs = [pair, shift(pair, "x", 1), shift(pair, "x", -1)]
    turned = shuffle(train, 2, 2, turned)
    sums, turned, far, near = hold((swap(sums, "zh", 0), turned, far, near))
    far = jnp.concatenate(far, axis=0)
    fars = [far, shift(far, "x", 1), shift(far, "x", -1)]
    turned = shuffle(train, 4, 2, turned)
    near_twins = [shift(piece, "core", 1) for piece in near]
    sums, turned, pairs, near, near_twins = hold(
        (swap(sums, "zh", 1), turned, pairs, near, near_twins)
    )
    pairs += forward(pairs[1], pairs[2], "x")
    out_blocks, in_blocks = inverses(sums, total_tokens)
    fars, out_blocks, pairs = hold((fars, out_blocks, pairs))
    fars += forward(fars[1], fars[2], "x")
    rest = pairs + fars
    pieces = near + rest + near_twins + [shift(piece, "core", 1) for piece in rest]

    count = query_owner.shape[0]
    here = block_ids()[:, None] == query_owner[None, :]
    pos = jnp.sum(jnp.where(here, jnp.arange(count, dtype=jnp.int32)[None, :], 0), axis=1)
    ordered = score(pieces, layout(), pos, turned, out_blocks, in_blocks)
    parts = lax.axis_size(SECTION)
    ordered = ordered.reshape(parts, ordered.shape[0] // parts, ordered.shape[1])
    arrived = lax.all_to_all(ordered, SECTION, split_axis=0, concat_axis=0, tiled=True)
    scores = jnp.sum(arrived.astype(jnp.float32), axis=0)

    examples = local_tokens // SEQ
    per_example = lax.dot_general(
        grads.reshape(examples, SEQ, RANK),
        acts.reshape(examples, SEQ, RANK),
        (((1,), (1,)), ((0,), (0,))),
        preferred_element_type=jnp.float32,
    )
    fresh_grads = (per_example / SEQ).reshape(1, examples, RANK * RANK).astype(jnp.bfloat16)
    return (fresh_grads, scores)


def solution(mesh):
    fine = jax.sharding.Mesh(
        mesh.devices.reshape(4, 4, 2, 2, 4), ("zh", "x", "core", "zl", "y")
    )
    placed = (
        P(SECTION, DP, None),
        P(SECTION, DP, None),
        P(SECTION, None, None),
        P(SECTION, None, None),
        P(SECTION, DP, None),
        P(SECTION, DP, None),
        P(),
    )
    return jax.shard_map(
        on_device,
        mesh=fine,
        in_specs=placed,
        out_specs=(P(SECTION, DP, None), P(SECTION, DP)),
        check_vma=False,
    )
```

```python
import functools

import jax
import jax.numpy as jnp
from jax import lax
from jax.experimental import pallas as pl
from jax.experimental.pallas import tpu as pltpu
from jax.sharding import PartitionSpec as P

SEQ = 256
RANK = 64
PITCH = 72
DP = ("zh", "x", "core")
SECTION = ("zl", "y")

VMEM_BYTES = 60 * 2**20
LIGHT = pl.CostEstimate(flops=0, bytes_accessed=1024, transcendentals=0)


def params():
    return pltpu.CompilerParams(vmem_limit_bytes=VMEM_BYTES)


def shuffle_kernel(t_ref, *refs):
    x_ref, wide = refs[-2:]
    for j in range(t_ref.shape[1] // 128):
        turned = t_ref[:, 128 * j : 128 * j + 128].astype(jnp.float32).T
        wide[PITCH * 2 * j : PITCH * 2 * j + RANK, :] = turned[:RANK, :]
        wide[PITCH * (2 * j + 1) : PITCH * (2 * j + 1) + RANK, :] = turned[RANK:, :]
    for i in range(RANK):
        x_ref[0, RANK * i : RANK * i + RANK, :] = wide[pl.ds(i, RANK, stride=PITCH), :].astype(
            jnp.bfloat16
        )


def shuffle(t, first, count, held=None):
    n, width = t.shape
    specs = [pl.BlockSpec((128, width), lambda j: (j + first, 0))]
    return pl.pallas_call(
        shuffle_kernel,
        grid=(count,),
        in_specs=specs + ([] if held is None else [pl.BlockSpec(memory_space=pl.ANY)]),
        out_specs=pl.BlockSpec((1, width, 128), lambda j: (j + first, 0, 0)),
        out_shape=jax.ShapeDtypeStruct((n // 128, width, 128), jnp.bfloat16),
        input_output_aliases={} if held is None else {1: 0},
        scratch_shapes=[pltpu.VMEM((RANK * PITCH, 128), jnp.float32)],
        compiler_params=params(),
        cost_estimate=LIGHT,
    )(*((t,) if held is None else (t, held)))


def weigh_kernel(x_ref, a_ref, b_ref, y_ref, low, high):
    a, b = a_ref[...], b_ref[...]
    width = x_ref.shape[1]
    for g in range(width // 256):
        band = slice(256 * g, 256 * g + 256)
        x = jnp.concatenate([x_ref[0, band, :], x_ref[1, band, :]], axis=1)
        y = jnp.dot(a, x, preferred_element_type=jnp.float32)
        for r in range(4):
            spot = slice(PITCH * (4 * g + r), PITCH * (4 * g + r) + RANK)
            low[spot, :] = y[RANK * r : RANK * r + RANK, :128]
            high[spot, :] = y[RANK * r : RANK * r + RANK, 128:]
    for g in range(width // 256):
        parts = []
        for k in range(4 * g, 4 * g + 4):
            pair = [half[pl.ds(k, RANK, stride=PITCH), :] for half in (low, high)]
            parts.append(jnp.concatenate(pair, axis=1).astype(jnp.bfloat16))
        z = jnp.concatenate(parts, axis=0)
        y_ref[0, 256 * g : 256 * g + 256, :] = jnp.dot(
            b, z, preferred_element_type=jnp.float32
        ).astype(jnp.bfloat16)


def weigh(x, a, b):
    chunks, width, _ = x.shape
    small = pl.BlockSpec((256, 256), lambda j: (0, 0))
    return pl.pallas_call(
        weigh_kernel,
        grid=(chunks // 2,),
        in_specs=[pl.BlockSpec((2, width, 128), lambda j: (j, 0, 0)), small, small],
        out_specs=pl.BlockSpec((1, width, 256), lambda j: (j, 0, 0)),
        out_shape=jax.ShapeDtypeStruct((chunks // 2, width, 256), jnp.bfloat16),
        scratch_shapes=[pltpu.VMEM((RANK * PITCH, 128), jnp.float32)] * 2,
        compiler_params=params(),
        cost_estimate=LIGHT,
    )(x, a, b)


def score_kernel(moves, count, pos_ref, w_ref, *refs):
    pieces, y_ref, rows, sems = refs[:count], refs[count], refs[count + 1], refs[count + 2]
    first = pl.program_id(0) == 0

    @pl.when(first)
    def _():
        copies = []
        for n, (piece, start) in enumerate(moves):
            place = pl.multiple_of(pos_ref[n] * 32, 32)
            copies.append(
                pltpu.make_async_copy(
                    pieces[piece].at[pl.ds(start, 32)], rows.at[pl.ds(place, 32)], sems.at[n]
                )
            )
        for copy in copies:
            copy.start()
        for copy in copies:
            copy.wait()

    for g in range(rows.shape[0] // 256):
        band = slice(256 * g, 256 * g + 256)
        y_ref[band, :] = jnp.dot(
            rows[band, :], w_ref[0], preferred_element_type=jnp.float32
        ).astype(jnp.bfloat16)


def score(pieces, pos, weighed):
    chunks, width, _ = weighed.shape
    moves = [(k, n) for k, piece in enumerate(pieces) for n in range(0, piece.shape[0], 32)]
    total = 32 * len(moves)
    return pl.pallas_call(
        functools.partial(score_kernel, moves, len(pieces)),
        grid=(chunks,),
        in_specs=[
            pl.BlockSpec(memory_space=pltpu.SMEM),
            pl.BlockSpec((1, width, 256), lambda j: (j, 0, 0)),
        ]
        + [pl.BlockSpec(memory_space=pl.ANY)] * len(pieces),
        out_specs=pl.BlockSpec((total, 256), lambda j: (0, j)),
        out_shape=jax.ShapeDtypeStruct((total, chunks * 256), jnp.bfloat16),
        scratch_shapes=[
            pltpu.VMEM((total, width), jnp.bfloat16),
            pltpu.SemaphoreType.DMA((len(moves),)),
        ],
        compiler_params=params(),
        cost_estimate=LIGHT,
    )(pos, weighed, *pieces)


def add_kernel(part_ref, out_ref):
    total = part_ref[0].astype(jnp.float32)
    for k in range(1, part_ref.shape[0]):
        total = total + part_ref[k].astype(jnp.float32)
    out_ref[...] = total


def add_parts(parts):
    count, rows, n = parts.shape
    return pl.pallas_call(
        add_kernel,
        grid=(2,),
        in_specs=[pl.BlockSpec((count, rows // 2, n), lambda j: (0, j, 0))],
        out_specs=pl.BlockSpec((rows // 2, n), lambda j: (j, 0)),
        out_shape=jax.ShapeDtypeStruct((rows, n), jnp.float32),
        compiler_params=params(),
        cost_estimate=LIGHT,
    )(parts)


def blocks(m):
    four=jnp.concatenate([m]*4,axis=1)
    four=jnp.concatenate([four]*4,axis=0)
    r=lax.broadcasted_iota(jnp.int32,four.shape,0)//RANK
    c=lax.broadcasted_iota(jnp.int32,four.shape,1)//RANK
    return jnp.where(r==c,four,0.0).astype(jnp.bfloat16)
def inverse_kernel(tokens, s_ref, a_ref, b_ref):
    m = s_ref[...] / tokens
    row = lax.broadcasted_iota(jnp.int32, m.shape, 0)
    lane = lax.broadcasted_iota(jnp.int32, m.shape, 1)
    left = lane < RANK
    lane = jnp.where(left, lane, lane - RANK)
    diag = jnp.where(row == lane, m, 0.0)
    mean_left = jnp.sum(jnp.where(left, diag, 0.0)) / RANK
    mean_right = jnp.sum(jnp.where(left, 0.0, diag)) / RANK
    mean = jnp.where(left, mean_left, mean_right)
    m = m / mean + jnp.where(row == lane, 0.1, 0.0)
    first = left[:1]
    pick = lambda r, k: jnp.where(first, r[:, k : k + 1], r[:, RANK + k : RANK + k + 1])
    for k in range(0, RANK, 2):
        r0, r1 = m[k : k + 1, :], m[k + 1 : k + 2, :]
        c0 = jnp.where(left, m[:, k : k + 1], m[:, RANK + k : RANK + k + 1])
        c1 = jnp.where(left, m[:, k + 1 : k + 2], m[:, RANK + k + 1 : RANK + k + 2])
        d00, d01, d10, d11 = pick(r0, k), pick(r0, k + 1), pick(r1, k), pick(r1, k + 1)
        scale = 1.0 / (d00 * d11 - d01 * d10)
        at0, at1 = lane[:1] == k, lane[:1] == k + 1
        r0 = jnp.where(at0, 1.0, jnp.where(at1, 0.0, r0))
        r1 = jnp.where(at1, 1.0, jnp.where(at0, 0.0, r1))
        s0 = (d11 * r0 - d01 * r1) * scale
        s1 = (d00 * r1 - d10 * r0) * scale
        kept = jnp.where((lane == k) | (lane == k + 1), 0.0, m)
        m = kept - c0 * s0 - c1 * s1
        m = jnp.where(row == k, s0, jnp.where(row == k + 1, s1, m))
    m = m / mean
    a_ref[...] = blocks(m[:, RANK:].T)
    b_ref[...] = blocks(m[:, :RANK])


def inverses(s,tokens):
    return pl.pallas_call(functools.partial(inverse_kernel,tokens),
        out_shape=[jax.ShapeDtypeStruct((256,256),jnp.bfloat16)]*2,
        cost_estimate=LIGHT,
    )(s)


def swap(value, axis, way):
    last = lax.axis_size(axis) - 1
    pairs = [(i, i ^ 1 if way == 0 else last - i) for i in range(last + 1)]
    return value + lax.ppermute(value, axis, pairs)


def twin(value):
    return lax.ppermute(value, "core", [(0, 1), (1, 0)])


def onward(value, axis):
    pairs = []
    for zh in range(4):
        for x in range(4):
            for core in range(2):
                step = 1 - 2 * core
                to = ((zh + step) % 4, x) if axis == "zh" else (zh, (x + step) % 4)
                pairs.append(((zh * 4 + x) * 2 + core, (to[0] * 4 + to[1]) * 2 + core))
    return lax.ppermute(value, DP, pairs)


def pack_kernel(first, second, third, out):
    out[:32, :] = first[...]
    out[32:64, :] = second[...]
    out[64:, :] = third[...]


def pack(*parts):
    return pl.pallas_call(
        pack_kernel,
        out_shape=jax.ShapeDtypeStruct((96, parts[0].shape[1]), parts[0].dtype),
        compiler_params=params(),
        cost_estimate=LIGHT,
    )(*parts)


def block_ids():
    zh, x, core = (lax.axis_index(axis) for axis in DP)
    near, back = 3 - 2 * core, 1 + 2 * core
    mine = [(near, 0), (near, 1), (2, 0)]
    theirs = [(back, 1), (back, 0), (2, 1)]
    runs = [(0, [(0, 0)]), (0, [(0, 1)])]
    runs += [(near, [(0, 0)]), (near, [(0, 1)]), (2, [(0, 0)])]
    runs += [(back, [(0, 1)]), (back, [(0, 0)]), (2, [(0, 1)])]
    runs += [(0, mine), (0, theirs), (near, mine), (near, theirs), (2, mine)]
    runs += [(back, theirs), (back, mine), (2, theirs)]
    ids = []
    for turn, blocks in runs:
        for climb, other in blocks:
            ids.append((((zh + climb) % 4) * 4 + (x + turn) % 4) * 2 + (core + other) % 2)
    return jnp.stack(ids)


def on_device(layer_inputs, output_grads, proj_in, proj_out, train_log, queries, query_owner):
    local_tokens = layer_inputs.shape[1]
    total_tokens = local_tokens * lax.axis_size(DP)
    hold = lax.optimization_barrier
    own, train = queries[0], train_log[0]
    other = twin(own)
    up, up_other = onward(own, "zh"), onward(other, "zh")
    near, near_other = onward(own, "x"), onward(other, "x")

    acts = jnp.dot(layer_inputs[0], proj_in[0], preferred_element_type=jnp.float32).astype(
        jnp.bfloat16
    )
    grads = jnp.dot(output_grads[0], proj_out[0], preferred_element_type=jnp.float32).astype(
        jnp.bfloat16
    )
    down = (((0,), (0,)), ((), ()))
    in_sum = lax.dot_general(acts, acts, down, preferred_element_type=jnp.float32)
    out_sum = lax.dot_general(grads, grads, down, preferred_element_type=jnp.float32)
    sums = swap(jnp.concatenate([in_sum, out_sum], axis=1), "core", 0)
    sums, train = hold((swap(sums, "x", 0), train))
    turned = shuffle(train, 0, 2)
    sums, turned, up, up_other, near = hold(
        (swap(sums, "x", 1), turned, up, up_other, near)
    )
    far, near_far = onward(up, "zh"), onward(near, "x")
    turned = shuffle(train, 2, 2, turned)
    turned = shuffle(train, 4, 2, turned)
    sums, turned, far, near_far, near_other = hold((sums, turned, far, near_far, near_other))
    mine = pack(up, up_other, far)
    theirs = twin(mine)
    side, side_other = onward(mine, "x"), onward(theirs, "x")
    sums = swap(swap(sums, "zh", 0), "zh", 1)
    sums, turned = hold((sums, turned))
    out_blocks, in_blocks = inverses(sums, total_tokens)
    ring = [near, near_other, near_far]
    ring_twins = [twin(piece) for piece in ring]
    out_blocks, side, side_other, ring_twins = hold((out_blocks, side, side_other, ring_twins))
    side_far = onward(side, "x")
    weighed = weigh(turned, out_blocks, in_blocks)
    wide = [side, side_other]
    wide_twins = [twin(piece) for piece in wide]
    weighed, side_far, wide_twins = hold((weighed, side_far, wide_twins))
    pieces = [own, other] + ring + ring_twins + [mine, theirs] + wide + [side_far]
    pieces += wide_twins + [twin(side_far)]

    count = query_owner.shape[0]
    here = block_ids()[:, None] == query_owner[None, :]
    pos = jnp.sum(jnp.where(here, jnp.arange(count, dtype=jnp.int32)[None, :], 0), axis=1)
    ordered = score(pieces, pos, weighed)
    parts = lax.axis_size(SECTION)
    ordered = ordered.reshape(parts, ordered.shape[0] // parts, ordered.shape[1])
    arrived = lax.all_to_all(ordered, SECTION, split_axis=0, concat_axis=0, tiled=True)
    scores = add_parts(arrived)

    examples = local_tokens // SEQ
    per_example = lax.dot_general(
        grads.reshape(examples, SEQ, RANK),
        acts.reshape(examples, SEQ, RANK),
        (((1,), (1,)), ((0,), (0,))),
        preferred_element_type=jnp.float32,
    )
    fresh_grads = (per_example / SEQ).reshape(1, examples, RANK * RANK).astype(jnp.bfloat16)
    return (fresh_grads, scores)


def solution(mesh):
    fine = jax.sharding.Mesh(
        mesh.devices.reshape(4, 4, 2, 2, 4), ("zh", "x", "core", "zl", "y")
    )
    placed = (
        P(SECTION, DP, None),
        P(SECTION, DP, None),
        P(SECTION, None, None),
        P(SECTION, None, None),
        P(SECTION, DP, None),
        P(SECTION, DP, None),
        P(),
    )
    return jax.shard_map(
        on_device,
        mesh=fine,
        in_specs=placed,
        out_specs=(P(SECTION, DP, None), P(SECTION, DP)),
        check_vma=False,
    )
```

```python
import functools

import jax
import jax.numpy as jnp
from jax import lax
from jax.experimental import pallas as pl
from jax.experimental.pallas import tpu as pltpu
from jax.sharding import PartitionSpec as P

SEQ = 256
RANK = 64
PITCH = 72
DP = ("zh", "x", "core")
SECTION = ("zl", "y")

VMEM_BYTES = 60 * 2**20
LIGHT = pl.CostEstimate(flops=0, bytes_accessed=1024, transcendentals=0)


def params():
    return pltpu.CompilerParams(vmem_limit_bytes=VMEM_BYTES)


def shuffle_kernel(t_ref, *refs):
    x_ref, wide = refs[-2:]
    for j in range(t_ref.shape[1] // 128):
        turned = t_ref[:, 128 * j : 128 * j + 128].astype(jnp.float32).T
        wide[PITCH * 2 * j : PITCH * 2 * j + RANK, :] = turned[:RANK, :]
        wide[PITCH * (2 * j + 1) : PITCH * (2 * j + 1) + RANK, :] = turned[RANK:, :]
    for i in range(RANK):
        x_ref[0, RANK * i : RANK * i + RANK, :] = wide[pl.ds(i, RANK, stride=PITCH), :].astype(
            jnp.bfloat16
        )


def shuffle(t, first, count, held=None):
    n, width = t.shape
    specs = [pl.BlockSpec((128, width), lambda j: (j + first, 0))]
    return pl.pallas_call(
        shuffle_kernel,
        grid=(count,),
        in_specs=specs + ([] if held is None else [pl.BlockSpec(memory_space=pl.ANY)]),
        out_specs=pl.BlockSpec((1, width, 128), lambda j: (j + first, 0, 0)),
        out_shape=jax.ShapeDtypeStruct((n // 128, width, 128), jnp.bfloat16),
        input_output_aliases={} if held is None else {1: 0},
        scratch_shapes=[pltpu.VMEM((RANK * PITCH, 128), jnp.float32)],
        compiler_params=params(),
        cost_estimate=LIGHT,
    )(*((t,) if held is None else (t, held)))


def weigh_kernel(x_ref, a_ref, b_ref, y_ref, low, high):
    a, b = a_ref[...], b_ref[...]
    width = x_ref.shape[1]
    for g in range(width // 256):
        band = slice(256 * g, 256 * g + 256)
        x = jnp.concatenate([x_ref[0, band, :], x_ref[1, band, :]], axis=1)
        y = jnp.dot(a, x, preferred_element_type=jnp.float32)
        for r in range(4):
            spot = slice(PITCH * (4 * g + r), PITCH * (4 * g + r) + RANK)
            low[spot, :] = y[RANK * r : RANK * r + RANK, :128]
            high[spot, :] = y[RANK * r : RANK * r + RANK, 128:]
    for g in range(width // 256):
        parts = []
        for k in range(4 * g, 4 * g + 4):
            pair = [half[pl.ds(k, RANK, stride=PITCH), :] for half in (low, high)]
            parts.append(jnp.concatenate(pair, axis=1).astype(jnp.bfloat16))
        z = jnp.concatenate(parts, axis=0)
        y_ref[0, 256 * g : 256 * g + 256, :] = jnp.dot(
            b, z, preferred_element_type=jnp.float32
        ).astype(jnp.bfloat16)


def weigh(x, a, b):
    chunks, width, _ = x.shape
    small = pl.BlockSpec((256, 256), lambda j: (0, 0))
    return pl.pallas_call(
        weigh_kernel,
        grid=(chunks // 2,),
        in_specs=[pl.BlockSpec((2, width, 128), lambda j: (j, 0, 0)), small, small],
        out_specs=pl.BlockSpec((1, width, 256), lambda j: (j, 0, 0)),
        out_shape=jax.ShapeDtypeStruct((chunks // 2, width, 256), jnp.bfloat16),
        scratch_shapes=[pltpu.VMEM((RANK * PITCH, 128), jnp.float32)] * 2,
        compiler_params=params(),
        cost_estimate=LIGHT,
    )(x, a, b)


def score_kernel(moves, count, pos_ref, w_ref, *refs):
    pieces, y_ref, rows, sems = refs[:count], refs[count], refs[count + 1], refs[count + 2]
    first = pl.program_id(0) == 0

    @pl.when(first)
    def _():
        copies = []
        for n, (piece, start) in enumerate(moves):
            place = pl.multiple_of(pos_ref[n] * 32, 32)
            copies.append(
                pltpu.make_async_copy(
                    pieces[piece].at[pl.ds(start, 32)], rows.at[pl.ds(place, 32)], sems.at[n]
                )
            )
        for copy in copies:
            copy.start()
        for copy in copies:
            copy.wait()

    for g in range(rows.shape[0] // 256):
        band = slice(256 * g, 256 * g + 256)
        y_ref[band, :] = jnp.dot(
            rows[band, :], w_ref[0], preferred_element_type=jnp.float32
        ).astype(jnp.bfloat16)


def score(pieces, pos, weighed):
    chunks, width, _ = weighed.shape
    moves = [(k, n) for k, piece in enumerate(pieces) for n in range(0, piece.shape[0], 32)]
    total = 32 * len(moves)
    return pl.pallas_call(
        functools.partial(score_kernel, moves, len(pieces)),
        grid=(chunks,),
        in_specs=[
            pl.BlockSpec(memory_space=pltpu.SMEM),
            pl.BlockSpec((1, width, 256), lambda j: (j, 0, 0)),
        ]
        + [pl.BlockSpec(memory_space=pl.ANY)] * len(pieces),
        out_specs=pl.BlockSpec((total, 256), lambda j: (0, j)),
        out_shape=jax.ShapeDtypeStruct((total, chunks * 256), jnp.bfloat16),
        scratch_shapes=[
            pltpu.VMEM((total, width), jnp.bfloat16),
            pltpu.SemaphoreType.DMA((len(moves),)),
        ],
        compiler_params=params(),
        cost_estimate=LIGHT,
    )(pos, weighed, *pieces)


def add_kernel(part_ref, out_ref):
    total = part_ref[0].astype(jnp.float32)
    for k in range(1, part_ref.shape[0]):
        total = total + part_ref[k].astype(jnp.float32)
    out_ref[...] = total


def add_parts(parts):
    count, rows, n = parts.shape
    return pl.pallas_call(
        add_kernel,
        grid=(2,),
        in_specs=[pl.BlockSpec((count, rows // 2, n), lambda j: (0, j, 0))],
        out_specs=pl.BlockSpec((rows // 2, n), lambda j: (j, 0)),
        out_shape=jax.ShapeDtypeStruct((rows, n), jnp.float32),
        compiler_params=params(),
        cost_estimate=LIGHT,
    )(parts)


def blocks(m):
    four=jnp.concatenate([m]*4,axis=1)
    four=jnp.concatenate([four]*4,axis=0)
    r=lax.broadcasted_iota(jnp.int32,four.shape,0)//RANK
    c=lax.broadcasted_iota(jnp.int32,four.shape,1)//RANK
    return jnp.where(r==c,four,0.0).astype(jnp.bfloat16)
def inverse_kernel(tokens, s_ref, a_ref, b_ref):
    m = s_ref[...] / tokens
    row = lax.broadcasted_iota(jnp.int32, m.shape, 0)
    lane = lax.broadcasted_iota(jnp.int32, m.shape, 1)
    left = lane < RANK
    lane = jnp.where(left, lane, lane - RANK)
    diag = jnp.where(row == lane, m, 0.0)
    mean_left = jnp.sum(jnp.where(left, diag, 0.0)) / RANK
    mean_right = jnp.sum(jnp.where(left, 0.0, diag)) / RANK
    mean = jnp.where(left, mean_left, mean_right)
    m = m / mean + jnp.where(row == lane, 0.1, 0.0)
    first = left[:1]
    pick = lambda r, k: jnp.where(first, r[:, k : k + 1], r[:, RANK + k : RANK + k + 1])
    for k in range(0, RANK, 2):
        r0, r1 = m[k : k + 1, :], m[k + 1 : k + 2, :]
        c0 = jnp.where(left, m[:, k : k + 1], m[:, RANK + k : RANK + k + 1])
        c1 = jnp.where(left, m[:, k + 1 : k + 2], m[:, RANK + k + 1 : RANK + k + 2])
        d00, d01, d10, d11 = pick(r0, k), pick(r0, k + 1), pick(r1, k), pick(r1, k + 1)
        scale = 1.0 / (d00 * d11 - d01 * d10)
        at0, at1 = lane[:1] == k, lane[:1] == k + 1
        r0 = jnp.where(at0, 1.0, jnp.where(at1, 0.0, r0))
        r1 = jnp.where(at1, 1.0, jnp.where(at0, 0.0, r1))
        s0 = (d11 * r0 - d01 * r1) * scale
        s1 = (d00 * r1 - d10 * r0) * scale
        kept = jnp.where((lane == k) | (lane == k + 1), 0.0, m)
        m = kept - c0 * s0 - c1 * s1
        m = jnp.where(row == k, s0, jnp.where(row == k + 1, s1, m))
    m = m / mean
    a_ref[...] = blocks(m[:, RANK:].T)
    b_ref[...] = blocks(m[:, :RANK])


def inverses(s,tokens):
    return pl.pallas_call(functools.partial(inverse_kernel,tokens),
        out_shape=[jax.ShapeDtypeStruct((256,256),jnp.bfloat16)]*2,
        cost_estimate=LIGHT,
    )(s)


def swap(value, axis, way):
    last = lax.axis_size(axis) - 1
    pairs = [(i, i ^ 1 if way == 0 else last - i) for i in range(last + 1)]
    return value + lax.ppermute(value, axis, pairs)


def twin(value):
    return lax.ppermute(value, "core", [(0, 1), (1, 0)])


def onward(value, axis):
    pairs = []
    for zh in range(4):
        for x in range(4):
            for core in range(2):
                step = 1 - 2 * core
                to = ((zh + step) % 4, x) if axis == "zh" else (zh, (x + step) % 4)
                pairs.append(((zh * 4 + x) * 2 + core, (to[0] * 4 + to[1]) * 2 + core))
    return lax.ppermute(value, DP, pairs)


def pack_kernel(first, second, out):
    out[:32, :] = first[...]
    out[32:, :] = second[...]


def pack(*parts):
    return pl.pallas_call(
        pack_kernel,
        out_shape=jax.ShapeDtypeStruct((64, parts[0].shape[1]), parts[0].dtype),
        compiler_params=params(),
        cost_estimate=LIGHT,
    )(*parts)


def block_ids():
    zh, x, core = (lax.axis_index(axis) for axis in DP)
    near, back = 3 - 2 * core, 1 + 2 * core
    mine, theirs = [(near, 0), (near, 1)], [(back, 1), (back, 0)]
    far, far_twin = [(2, 0)], [(2, 1)]
    runs = [(0, [(0, 0)]), (0, [(0, 1)])]
    runs += [(near, [(0, 0)]), (near, [(0, 1)]), (2, [(0, 0)])]
    runs += [(back, [(0, 1)]), (back, [(0, 0)]), (2, [(0, 1)])]
    runs += [(0, mine), (0, theirs), (0, far), (0, far_twin)]
    runs += [(near, mine), (near, theirs), (near, far), (near, far_twin)]
    runs += [(back, theirs), (back, mine), (back, far_twin), (back, far)]
    runs += [(2, mine), (2, far), (2, theirs), (2, far_twin)]
    ids = []
    for turn, blocks in runs:
        for climb, other in blocks:
            ids.append((((zh + climb) % 4) * 4 + (x + turn) % 4) * 2 + (core + other) % 2)
    return jnp.stack(ids)


def on_device(layer_inputs, output_grads, proj_in, proj_out, train_log, queries, query_owner):
    local_tokens = layer_inputs.shape[1]
    total_tokens = local_tokens * lax.axis_size(DP)
    hold = lax.optimization_barrier
    own, train = queries[0], train_log[0]
    other = twin(own)
    up, up_other = onward(own, "zh"), onward(other, "zh")
    near, near_other = onward(own, "x"), onward(other, "x")

    acts = jnp.dot(layer_inputs[0], proj_in[0], preferred_element_type=jnp.float32).astype(
        jnp.bfloat16
    )
    grads = jnp.dot(output_grads[0], proj_out[0], preferred_element_type=jnp.float32).astype(
        jnp.bfloat16
    )
    down = (((0,), (0,)), ((), ()))
    in_sum = lax.dot_general(acts, acts, down, preferred_element_type=jnp.float32)
    out_sum = lax.dot_general(grads, grads, down, preferred_element_type=jnp.float32)
    sums = swap(jnp.concatenate([in_sum, out_sum], axis=1), "core", 0)
    count = query_owner.shape[0]
    here = block_ids()[:, None] == query_owner[None, :]
    pos = jnp.sum(jnp.where(here, jnp.arange(count, dtype=jnp.int32)[None, :], 0), axis=1)
    sums, train, pos = hold((swap(sums, "x", 0), train, pos))
    turned = shuffle(train, 0, 2)
    sums, turned, up, up_other, near = hold(
        (swap(sums, "x", 1), turned, up, up_other, near)
    )
    far, near_far = onward(up, "zh"), onward(near, "x")
    pair = pack(up, up_other)
    pair_twin = twin(pair)
    side, side_other = onward(pair, "x"), onward(pair_twin, "x")
    sums = swap(sums, "zh", 0)
    turned = shuffle(train, 2, 2, turned)
    turned = shuffle(train, 4, 2, turned)
    sums, turned, far, near_far, near_other = hold((sums, turned, far, near_far, near_other))
    far_twin = twin(far)
    far_side, far_side_other = onward(far, "x"), onward(far_twin, "x")
    sums, side = hold((swap(sums, "zh", 1), side))
    side_far = onward(side, "x")
    out_blocks, in_blocks = inverses(sums, total_tokens)
    ring = [near, near_other, near_far]
    ring_twins = [twin(piece) for piece in ring]
    out_blocks, far_side, far_side_other, side_other, ring_twins = hold(
        (out_blocks, far_side, far_side_other, side_other, ring_twins)
    )
    last = [side_far, onward(far_side, "x")]
    weighed = weigh(turned, out_blocks, in_blocks)
    wide = [side, side_other, far_side, far_side_other]
    wide_twins = [twin(piece) for piece in wide]
    weighed, last, wide_twins = hold((weighed, last, wide_twins))
    pieces = [own, other] + ring + ring_twins + [pair, pair_twin, far, far_twin]
    pieces += wide + wide_twins + last + [twin(piece) for piece in last]

    ordered = score(pieces, pos, weighed)
    parts = lax.axis_size(SECTION)
    ordered = ordered.reshape(parts, ordered.shape[0] // parts, ordered.shape[1])
    arrived = lax.all_to_all(ordered, SECTION, split_axis=0, concat_axis=0, tiled=True)
    scores = add_parts(arrived)

    examples = local_tokens // SEQ
    per_example = lax.dot_general(
        grads.reshape(examples, SEQ, RANK),
        acts.reshape(examples, SEQ, RANK),
        (((1,), (1,)), ((0,), (0,))),
        preferred_element_type=jnp.float32,
    )
    fresh_grads = (per_example / SEQ).reshape(1, examples, RANK * RANK).astype(jnp.bfloat16)
    return (fresh_grads, scores)


def solution(mesh):
    fine = jax.sharding.Mesh(
        mesh.devices.reshape(4, 4, 2, 2, 4), ("zh", "x", "core", "zl", "y")
    )
    placed = (
        P(SECTION, DP, None),
        P(SECTION, DP, None),
        P(SECTION, None, None),
        P(SECTION, None, None),
        P(SECTION, DP, None),
        P(SECTION, DP, None),
        P(),
    )
    return jax.shard_map(
        on_device,
        mesh=fine,
        in_specs=placed,
        out_specs=(P(SECTION, DP, None), P(SECTION, DP)),
        check_vma=False,
    )
```

```python
import functools

import jax
import jax.numpy as jnp
from jax import lax
from jax.experimental import pallas as pl
from jax.experimental.pallas import tpu as pltpu
from jax.sharding import PartitionSpec as P

SEQ = 256
RANK = 64
PITCH = 72
DP = ("zh", "x", "core")
SECTION = ("zl", "y")

VMEM_BYTES = 60 * 2**20
LIGHT = pl.CostEstimate(flops=0, bytes_accessed=1024, transcendentals=0)


def params():
    return pltpu.CompilerParams(vmem_limit_bytes=VMEM_BYTES)


def shuffle_kernel(t_ref, *refs):
    x_ref, wide = refs[-2:]
    for j in range(t_ref.shape[1] // 128):
        turned = t_ref[:, 128 * j : 128 * j + 128].astype(jnp.float32).T
        wide[PITCH * 2 * j : PITCH * 2 * j + RANK, :] = turned[:RANK, :]
        wide[PITCH * (2 * j + 1) : PITCH * (2 * j + 1) + RANK, :] = turned[RANK:, :]
    for i in range(RANK):
        x_ref[0, RANK * i : RANK * i + RANK, :] = wide[pl.ds(i, RANK, stride=PITCH), :].astype(
            jnp.bfloat16
        )


def shuffle(t, first, count, held=None):
    n, width = t.shape
    specs = [pl.BlockSpec((128, width), lambda j: (j + first, 0))]
    return pl.pallas_call(
        shuffle_kernel,
        grid=(count,),
        in_specs=specs + ([] if held is None else [pl.BlockSpec(memory_space=pl.ANY)]),
        out_specs=pl.BlockSpec((1, width, 128), lambda j: (j + first, 0, 0)),
        out_shape=jax.ShapeDtypeStruct((n // 128, width, 128), jnp.bfloat16),
        input_output_aliases={} if held is None else {1: 0},
        scratch_shapes=[pltpu.VMEM((RANK * PITCH, 128), jnp.float32)],
        compiler_params=params(),
        cost_estimate=LIGHT,
    )(*((t,) if held is None else (t, held)))


def weigh_kernel(x_ref, a_ref, b_ref, y_ref, low, high):
    a, b = a_ref[...], b_ref[...]
    width = x_ref.shape[1]
    for g in range(width // 256):
        band = slice(256 * g, 256 * g + 256)
        x = jnp.concatenate([x_ref[0, band, :], x_ref[1, band, :]], axis=1)
        y = jnp.dot(a, x, preferred_element_type=jnp.float32)
        for r in range(4):
            spot = slice(PITCH * (4 * g + r), PITCH * (4 * g + r) + RANK)
            low[spot, :] = y[RANK * r : RANK * r + RANK, :128]
            high[spot, :] = y[RANK * r : RANK * r + RANK, 128:]
    for g in range(width // 256):
        parts = []
        for k in range(4 * g, 4 * g + 4):
            pair = [half[pl.ds(k, RANK, stride=PITCH), :] for half in (low, high)]
            parts.append(jnp.concatenate(pair, axis=1).astype(jnp.bfloat16))
        z = jnp.concatenate(parts, axis=0)
        y_ref[0, 256 * g : 256 * g + 256, :] = jnp.dot(
            b, z, preferred_element_type=jnp.float32
        ).astype(jnp.bfloat16)


def weigh(x, a, b):
    chunks, width, _ = x.shape
    small = pl.BlockSpec((256, 256), lambda j: (0, 0))
    return pl.pallas_call(
        weigh_kernel,
        grid=(chunks // 2,),
        in_specs=[pl.BlockSpec((2, width, 128), lambda j: (j, 0, 0)), small, small],
        out_specs=pl.BlockSpec((1, width, 256), lambda j: (j, 0, 0)),
        out_shape=jax.ShapeDtypeStruct((chunks // 2, width, 256), jnp.bfloat16),
        scratch_shapes=[pltpu.VMEM((RANK * PITCH, 128), jnp.float32)] * 2,
        compiler_params=params(),
        cost_estimate=LIGHT,
    )(x, a, b)


def score_kernel(moves, count, pos_ref, w_ref, *refs):
    pieces, y_ref = refs[:count], refs[count]
    rows, partial, sems = refs[count + 1 :]
    half = rows.shape[1] // 2
    first = pl.program_id(0) == 0
    bands = [slice(256 * g, 256 * g + 256) for g in range(rows.shape[0] // 256)]

    def dot(band, depth):
        return jnp.dot(
            rows[band, depth], w_ref[0, depth, :], preferred_element_type=jnp.float32
        )

    @pl.when(first)
    def _():
        sides = []
        for side in range(2):
            columns = pl.ds(side * half, half)
            copies = []
            for n, (piece, start) in enumerate(moves):
                place = pl.multiple_of(pos_ref[n] * 32, 32)
                copies.append(
                    pltpu.make_async_copy(
                        pieces[piece].at[pl.ds(start, 32), columns],
                        rows.at[pl.ds(place, 32), columns],
                        sems.at[side * len(moves) + n],
                    )
                )
            sides.append(copies)
        for copy in sides[0] + sides[1]:
            copy.start()
        for copy in sides[0]:
            copy.wait()
        for band in bands:
            partial[band, :] = dot(band, slice(0, half))
        for copy in sides[1]:
            copy.wait()
        for band in bands:
            total = partial[band, :] + dot(band, slice(half, 2 * half))
            y_ref[band, :] = total.astype(jnp.bfloat16)

    @pl.when(jnp.logical_not(first))
    def _():
        for band in bands:
            y_ref[band, :] = dot(band, slice(0, 2 * half)).astype(jnp.bfloat16)


def score(pieces, pos, weighed):
    chunks, width, _ = weighed.shape
    moves = [(k, n) for k, piece in enumerate(pieces) for n in range(0, piece.shape[0], 32)]
    total = 32 * len(moves)
    return pl.pallas_call(
        functools.partial(score_kernel, moves, len(pieces)),
        grid=(chunks,),
        in_specs=[
            pl.BlockSpec(memory_space=pltpu.SMEM),
            pl.BlockSpec((1, width, 256), lambda j: (j, 0, 0)),
        ]
        + [pl.BlockSpec(memory_space=pl.ANY)] * len(pieces),
        out_specs=pl.BlockSpec((total, 256), lambda j: (0, j)),
        out_shape=jax.ShapeDtypeStruct((total, chunks * 256), jnp.bfloat16),
        scratch_shapes=[
            pltpu.VMEM((total, width), jnp.bfloat16),
            pltpu.VMEM((total, 256), jnp.float32),
            pltpu.SemaphoreType.DMA((2 * len(moves),)),
        ],
        compiler_params=params(),
        cost_estimate=LIGHT,
    )(pos, weighed, *pieces)


def add_kernel(part_ref, out_ref):
    total = part_ref[0].astype(jnp.float32)
    for k in range(1, part_ref.shape[0]):
        total = total + part_ref[k].astype(jnp.float32)
    out_ref[...] = total


def add_parts(parts):
    count, rows, n = parts.shape
    return pl.pallas_call(
        add_kernel,
        grid=(2,),
        in_specs=[pl.BlockSpec((count, rows // 2, n), lambda j: (0, j, 0))],
        out_specs=pl.BlockSpec((rows // 2, n), lambda j: (j, 0)),
        out_shape=jax.ShapeDtypeStruct((rows, n), jnp.float32),
        compiler_params=params(),
        cost_estimate=LIGHT,
    )(parts)


def blocks(m):
    four=jnp.concatenate([m]*4,axis=1)
    four=jnp.concatenate([four]*4,axis=0)
    r=lax.broadcasted_iota(jnp.int32,four.shape,0)//RANK
    c=lax.broadcasted_iota(jnp.int32,four.shape,1)//RANK
    return jnp.where(r==c,four,0.0).astype(jnp.bfloat16)
def inverse_kernel(tokens, s_ref, a_ref, b_ref):
    m = s_ref[...] / tokens
    row = lax.broadcasted_iota(jnp.int32, m.shape, 0)
    lane = lax.broadcasted_iota(jnp.int32, m.shape, 1)
    left = lane < RANK
    lane = jnp.where(left, lane, lane - RANK)
    diag = jnp.where(row == lane, m, 0.0)
    mean_left = jnp.sum(jnp.where(left, diag, 0.0)) / RANK
    mean_right = jnp.sum(jnp.where(left, 0.0, diag)) / RANK
    mean = jnp.where(left, mean_left, mean_right)
    m = m / mean + jnp.where(row == lane, 0.1, 0.0)
    first = left[:1]
    pick = lambda r, k: jnp.where(first, r[:, k : k + 1], r[:, RANK + k : RANK + k + 1])
    for k in range(0, RANK, 2):
        r0, r1 = m[k : k + 1, :], m[k + 1 : k + 2, :]
        c0 = jnp.where(left, m[:, k : k + 1], m[:, RANK + k : RANK + k + 1])
        c1 = jnp.where(left, m[:, k + 1 : k + 2], m[:, RANK + k + 1 : RANK + k + 2])
        d00, d01, d10, d11 = pick(r0, k), pick(r0, k + 1), pick(r1, k), pick(r1, k + 1)
        scale = 1.0 / (d00 * d11 - d01 * d10)
        at0, at1 = lane[:1] == k, lane[:1] == k + 1
        r0 = jnp.where(at0, 1.0, jnp.where(at1, 0.0, r0))
        r1 = jnp.where(at1, 1.0, jnp.where(at0, 0.0, r1))
        s0 = (d11 * r0 - d01 * r1) * scale
        s1 = (d00 * r1 - d10 * r0) * scale
        kept = jnp.where((lane == k) | (lane == k + 1), 0.0, m)
        m = kept - c0 * s0 - c1 * s1
        m = jnp.where(row == k, s0, jnp.where(row == k + 1, s1, m))
    m = m / mean
    a_ref[...] = blocks(m[:, RANK:].T)
    b_ref[...] = blocks(m[:, :RANK])


def inverses(s,tokens):
    return pl.pallas_call(functools.partial(inverse_kernel,tokens),
        out_shape=[jax.ShapeDtypeStruct((256,256),jnp.bfloat16)]*2,
        cost_estimate=LIGHT,
    )(s)


def swap(value, axis, way):
    last = lax.axis_size(axis) - 1
    pairs = [(i, i ^ 1 if way == 0 else last - i) for i in range(last + 1)]
    return value + lax.ppermute(value, axis, pairs)


def twin(value):
    return lax.ppermute(value, "core", [(0, 1), (1, 0)])


def onward(value, axis):
    pairs = []
    for zh in range(4):
        for x in range(4):
            for core in range(2):
                step = 1 - 2 * core
                to = ((zh + step) % 4, x) if axis == "zh" else (zh, (x + step) % 4)
                pairs.append(((zh * 4 + x) * 2 + core, (to[0] * 4 + to[1]) * 2 + core))
    return lax.ppermute(value, DP, pairs)


def pack_kernel(first, second, out):
    out[:32, :] = first[...]
    out[32:, :] = second[...]


def pack(*parts):
    return pl.pallas_call(
        pack_kernel,
        out_shape=jax.ShapeDtypeStruct((64, parts[0].shape[1]), parts[0].dtype),
        compiler_params=params(),
        cost_estimate=LIGHT,
    )(*parts)


def block_ids():
    zh, x, core = (lax.axis_index(axis) for axis in DP)
    near, back = 3 - 2 * core, 1 + 2 * core
    mine, theirs = [(near, 0), (near, 1)], [(back, 1), (back, 0)]
    far, far_twin = [(2, 0)], [(2, 1)]
    runs = [(0, [(0, 0)]), (0, [(0, 1)])]
    runs += [(near, [(0, 0)]), (near, [(0, 1)]), (2, [(0, 0)])]
    runs += [(back, [(0, 1)]), (back, [(0, 0)]), (2, [(0, 1)])]
    runs += [(0, mine), (0, theirs), (0, far), (0, far_twin)]
    runs += [(near, mine), (near, theirs), (near, far), (near, far_twin)]
    runs += [(back, theirs), (back, mine), (back, far_twin), (back, far)]
    runs += [(2, mine), (2, far), (2, theirs), (2, far_twin)]
    ids = []
    for turn, blocks in runs:
        for climb, other in blocks:
            ids.append((((zh + climb) % 4) * 4 + (x + turn) % 4) * 2 + (core + other) % 2)
    return jnp.stack(ids)


def on_device(layer_inputs, output_grads, proj_in, proj_out, train_log, queries, query_owner):
    local_tokens = layer_inputs.shape[1]
    total_tokens = local_tokens * lax.axis_size(DP)
    hold = lax.optimization_barrier
    own, train = queries[0], train_log[0]
    other = twin(own)
    up, up_other = onward(own, "zh"), onward(other, "zh")
    near, near_other = onward(own, "x"), onward(other, "x")

    acts = jnp.dot(layer_inputs[0], proj_in[0], preferred_element_type=jnp.float32).astype(
        jnp.bfloat16
    )
    grads = jnp.dot(output_grads[0], proj_out[0], preferred_element_type=jnp.float32).astype(
        jnp.bfloat16
    )
    down = (((0,), (0,)), ((), ()))
    in_sum = lax.dot_general(acts, acts, down, preferred_element_type=jnp.float32)
    out_sum = lax.dot_general(grads, grads, down, preferred_element_type=jnp.float32)
    sums = swap(jnp.concatenate([in_sum, out_sum], axis=1), "core", 0)
    count = query_owner.shape[0]
    here = block_ids()[:, None] == query_owner[None, :]
    pos = jnp.sum(jnp.where(here, jnp.arange(count, dtype=jnp.int32)[None, :], 0), axis=1)
    sums, train, pos = hold((swap(sums, "x", 0), train, pos))
    turned = shuffle(train, 0, 2)
    sums, turned, up, up_other, near = hold(
        (swap(sums, "x", 1), turned, up, up_other, near)
    )
    far, near_far = onward(up, "zh"), onward(near, "x")
    pair = pack(up, up_other)
    pair_twin = twin(pair)
    side, side_other = onward(pair, "x"), onward(pair_twin, "x")
    sums = swap(sums, "zh", 0)
    turned = shuffle(train, 2, 2, turned)
    turned = shuffle(train, 4, 2, turned)
    sums, turned, far, near_far, near_other = hold((sums, turned, far, near_far, near_other))
    far_twin = twin(far)
    far_side, far_side_other = onward(far, "x"), onward(far_twin, "x")
    sums, side = hold((swap(sums, "zh", 1), side))
    side_far = onward(side, "x")
    out_blocks, in_blocks = inverses(sums, total_tokens)
    ring = [near, near_other, near_far]
    ring_twins = [twin(piece) for piece in ring]
    out_blocks, far_side, far_side_other, side_other, ring_twins = hold(
        (out_blocks, far_side, far_side_other, side_other, ring_twins)
    )
    last = [side_far, onward(far_side, "x")]
    weighed = weigh(turned, out_blocks, in_blocks)
    wide = [side, side_other, far_side, far_side_other]
    wide_twins = [twin(piece) for piece in wide]
    weighed, last, wide_twins = hold((weighed, last, wide_twins))
    pieces = [own, other] + ring + ring_twins + [pair, pair_twin, far, far_twin]
    pieces += wide + wide_twins + last + [twin(piece) for piece in last]

    ordered = score(pieces, pos, weighed)
    parts = lax.axis_size(SECTION)
    ordered = ordered.reshape(parts, ordered.shape[0] // parts, ordered.shape[1])
    arrived = lax.all_to_all(ordered, SECTION, split_axis=0, concat_axis=0, tiled=True)
    scores = add_parts(arrived)

    examples = local_tokens // SEQ
    per_example = lax.dot_general(
        grads.reshape(examples, SEQ, RANK),
        acts.reshape(examples, SEQ, RANK),
        (((1,), (1,)), ((0,), (0,))),
        preferred_element_type=jnp.float32,
    )
    fresh_grads = (per_example / SEQ).reshape(1, examples, RANK * RANK).astype(jnp.bfloat16)
    return (fresh_grads, scores)


def solution(mesh):
    fine = jax.sharding.Mesh(
        mesh.devices.reshape(4, 4, 2, 2, 4), ("zh", "x", "core", "zl", "y")
    )
    placed = (
        P(SECTION, DP, None),
        P(SECTION, DP, None),
        P(SECTION, None, None),
        P(SECTION, None, None),
        P(SECTION, DP, None),
        P(SECTION, DP, None),
        P(),
    )
    return jax.shard_map(
        on_device,
        mesh=fine,
        in_specs=placed,
        out_specs=(P(SECTION, DP, None), P(SECTION, DP)),
        check_vma=False,
    )
```
